256 devices in a mesh: dp: 16 (over y, z_hi), tensor: 16 (over x, z_lo, core).
Axes of the slice: x: 4, y: 4, z: 8 (z_hi: 4, z_lo: 2; z = z_hi * 2 + z_lo), core: 2. Of those that a mesh axis runs over, the one named last changes fastest.
Arguments:
- grad_parts: bfloat16 [16, 16, 4096, 768], P('dp', None, 'tensor'), may hold values from -1500 to 1500
- momentum: bfloat16 [16, 4096, 768], P('dp', 'tensor'), may hold values from -1500 to 1500
Outputs:
- update: bfloat16 [16, 4096, 768], P(None, 'tensor')
- new_momentum: bfloat16 [16, 4096, 768], P('dp', 'tensor')
The draws below stay inside these ranges and needn't reach their ends.
All inputs are finite; a program needn't handle non-finite values.
Results may differ from the reference program's by a relative error of at most 0.001.
Values may be sent and summed in bfloat16 or wider, within the bound.
No kernel may reach another device: no remote copies, remote signals or barrier semaphores. Data moves between devices by JAX's collectives and lax.ppermute only.
A program may use at most 128 MiB of HBM per device.

```python
import math
import jax
import jax.numpy as jnp
from jax import lax

ROWS = 4096
COLS = 768
ITERS = 3
EXPERTS = 16
PARTIALS = 16


def matrix_scales(key):
    row_key = jax.random.fold_in(key, 100)
    col_key = jax.random.fold_in(key, 101)
    log_span = math.log(10.0)
    row_scale = jnp.exp(jax.random.uniform(row_key, (EXPERTS, ROWS, 1), jnp.float32, 0.0, log_span))
    col_scale = jnp.exp(jax.random.uniform(col_key, (EXPERTS, 1, COLS), jnp.float32, 0.0, log_span))
    return (row_scale, col_scale)


def shared_direction(key):
    left_key = jax.random.fold_in(key, 102)
    right_key = jax.random.fold_in(key, 103)
    left_factor = jax.random.uniform(left_key, (EXPERTS, ROWS, 4), jnp.float32, -1.7, 1.7)
    right_factor = jax.random.uniform(right_key, (EXPERTS, 4, COLS), jnp.float32, -1.7, 1.7)
    summed_terms = jnp.zeros((EXPERTS, ROWS, COLS), jnp.float32)
    for rank_index in range(4):
        summed_terms = summed_terms + left_factor[:, :, rank_index:rank_index + 1] * right_factor[:, rank_index:rank_index + 1, :]
    return 0.5 * summed_terms


def draw_grad_parts(key, part):
    row_scale, col_scale = matrix_scales(key)
    low_rank = shared_direction(key)
    key = jax.random.fold_in(key, 3)
    noise_key, pair_key = jax.random.split(key, 2)
    full_shape = (PARTIALS, EXPERTS, ROWS, COLS)
    own_part = jax.random.uniform(noise_key, full_shape, jnp.float32, -1.7, 1.7)
    entries = own_part + 0.6 / math.sqrt(PARTIALS) * low_rank[None]
    pair_scale = jnp.exp(jax.random.uniform(pair_key, (PARTIALS, EXPERTS, 1, 1), jnp.float32, math.log(0.5), math.log(2.0)))
    return (entries * pair_scale * row_scale[None] * col_scale[None]).astype(jnp.bfloat16)


def draw_momentum(key, part):
    row_scale, col_scale = matrix_scales(key)
    low_rank = shared_direction(key)
    key = jax.random.fold_in(key, 5)
    full_shape = (EXPERTS, ROWS, COLS)
    entries = jax.random.uniform(key, full_shape, jnp.float32, -1.7, 1.7)
    return ((3.0 * entries + 1.5 * low_rank) * row_scale * col_scale).astype(jnp.bfloat16)


def setup_inputs(seed: int = 0) -> dict:
    seeds = jax.random.split(jax.random.key(seed), 3)
    return {
        "grad_parts": draw_grad_parts(jax.random.fold_in(seeds[2], 71), 0),
        "momentum": draw_momentum(jax.random.fold_in(seeds[2], 71), 0),
    }


momentum_decay = 0.95
epsilon = 1e-07
first_coef = 3.4445
third_coef = -4.775
fifth_coef = 2.0315
highest = lax.Precision.HIGHEST

def newton_schulz(blended):
    norm_total = jnp.sum(blended * blended)
    inverse_norm = 1.0 / (jnp.sqrt(norm_total) + epsilon)
    current = blended * inverse_norm
    for iteration in range(ITERS):
        gram_matrix = jnp.dot(current.T, current, precision=highest, preferred_element_type=jnp.float32)
        squared = jnp.dot(gram_matrix, gram_matrix, precision=highest, preferred_element_type=jnp.float32)
        polynomial = third_coef * gram_matrix + fifth_coef * squared
        current = first_coef * current + jnp.dot(current, polynomial, precision=highest, preferred_element_type=jnp.float32)
    return current

def reference(grad_parts, momentum):

    def one_expert(expert_index):
        partials = lax.dynamic_index_in_dim(grad_parts, expert_index, 1, keepdims=False)
        summed = lax.optimization_barrier(jnp.sum(partials.astype(jnp.float32), axis=0))
        previous = lax.dynamic_index_in_dim(momentum, expert_index, 0, keepdims=False)
        velocity = momentum_decay * previous.astype(jnp.float32) + summed
        blended = summed + momentum_decay * velocity
        final = newton_schulz(blended)
        update = (final * math.sqrt(ROWS)).astype(jnp.bfloat16)
        return (update, velocity.astype(jnp.bfloat16))
    update, new_momentum = lax.map(one_expert, jnp.arange(EXPERTS, dtype=jnp.int32))
    return (update, new_momentum)
```

```python
import math

import jax
import jax.numpy as jnp
from jax import lax
from jax.experimental import pallas as pl
from jax.experimental.pallas import tpu as pltpu
from jax.sharding import PartitionSpec as P

ITERS = 3
NY, NZ = 4, 4
NX = 4

momentum_decay = 0.95
epsilon = 1e-07
first_coef = 3.4445
third_coef = -4.775
fifth_coef = 2.0315
f32 = jnp.float32
bf16 = jnp.bfloat16
BLK = 256
PAIRS = ((0, 0), (0, 1), (1, 1), (0, 2), (1, 2), (2, 2))

Y_PERM = {k: [(y * NZ + z, (y + k) % NY * NZ + z) for y in range(NY) for z in range(NZ)] for k in (1, 2, 3)}
Z_PERM = {k: [(y * NZ + z, y * NZ + (z + k) % NZ) for y in range(NY) for z in range(NZ)] for k in (1, 2, 3)}
X_PERM = {k: [(t, (t + 4 * k) % 16) for t in range(16)] for k in (1, 2, 3)}
CORE_PERM = [(t, t ^ 1) for t in range(16)]
ZLO_PERM = [(t, t ^ 2) for t in range(16)]


def to_y(value, k):
    return lax.ppermute(value, "dp", Y_PERM[k % NY])


def to_z(value, k):
    return lax.ppermute(value, "dp", Z_PERM[k % NZ])


def to_x(value, k):
    return lax.ppermute(value, "tensor", X_PERM[k % NX])


def split(value):
    hi = value.astype(bf16)
    lo = (value - hi.astype(f32)).astype(bf16)
    return hi, lo


def dot(a, b, contract=((1,), (0,))):
    return lax.dot_general(a, b, (contract, ((), ())), preferred_element_type=f32)


def product(a, b, contract=((1,), (0,))):
    return dot(a[0], b[0], contract) + (dot(a[0], b[1], contract) + dot(a[1], b[0], contract))


def gram_kernel(s_ref, r1_ref, r3_ref, m_ref, b_ref, nm_ref, g_ref):
    summed = s_ref[...] + r1_ref[...] + r3_ref[...]
    velocity = momentum_decay * m_ref[...].astype(f32) + summed
    nm_ref[...] = velocity.astype(bf16)
    blended = summed + momentum_decay * velocity
    b_ref[...] = blended
    hi, lo = split(blended)
    rows = ((0,), (0,))
    for n, (i, j) in enumerate(PAIRS):
        at, to = slice(i * BLK, (i + 1) * BLK), slice(j * BLK, (j + 1) * BLK)
        g_ref[n] = product((hi[:, at], lo[:, at]), (hi[:, to], lo[:, to]), rows)


def chain_kernel(rows, c_ref, mine_ref, other_ref, b_ref, out_ref, g_ref, gh_ref, gl_ref, qh_ref, ql_ref, sh_ref, sl_ref):
    size = 3 * BLK
    first = c_ref[0] == 0
    diagonal = lax.broadcasted_iota(jnp.int32, (BLK, BLK), 0) == lax.broadcasted_iota(jnp.int32, (BLK, BLK), 1)
    blocks = []
    trace = jnp.zeros((1, 1), f32)
    for n, (i, j) in enumerate(PAIRS):
        mine, other = mine_ref[n % 3], other_ref[n % 3]
        block = jnp.where(first, mine, other) if n < 3 else jnp.where(first, other, mine)
        blocks.append(block)
        if i == j:
            trace += jnp.sum(jnp.where(diagonal, block, 0.0), keepdims=True)
    inverse = 1.0 / (jnp.sqrt(trace) + epsilon)
    squared_inverse = inverse * inverse
    for n, (i, j) in enumerate(PAIRS):
        block = blocks[n] * squared_inverse
        at, to = slice(i * BLK, (i + 1) * BLK), slice(j * BLK, (j + 1) * BLK)
        g_ref[at, to] = block
        gh_ref[at, to], gl_ref[at, to] = split(block)
        if i != j:
            block = block.T
            g_ref[to, at] = block
            gh_ref[to, at], gl_ref[to, at] = split(block)
    x = b_ref[...] * inverse
    for iteration in range(ITERS):
        last = iteration == ITERS - 1

        @pl.loop(0, 3)
        def _(n):
            at = pl.ds(pl.multiple_of(n * BLK, BLK), BLK)
            squared = product((gh_ref[at], gl_ref[at]), (gh_ref[...], gl_ref[...]))
            r = lax.broadcasted_iota(jnp.int32, (BLK, size), 0) + n * BLK
            eye = r == lax.broadcasted_iota(jnp.int32, (BLK, size), 1)
            q = third_coef * g_ref[at] + fifth_coef * squared + jnp.where(eye, first_coef, 0.0)
            qh_ref[at], ql_ref[at] = split(q)

        x = product(split(x), (qh_ref[...], ql_ref[...]))
        if not last:

            @pl.loop(0, 3)
            def _(n):
                at = pl.ds(pl.multiple_of(n * BLK, BLK), BLK)
                s = product((gh_ref[at], gl_ref[at]), (qh_ref[...], ql_ref[...]))
                sh_ref[at], sl_ref[at] = split(s)

            @pl.loop(0, 3)
            def _(n):
                at = pl.ds(pl.multiple_of(n * BLK, BLK), BLK)
                g = product((sh_ref[at], sl_ref[at]), (qh_ref[...], ql_ref[...]))
                g_ref[at] = g
                gh_ref[at], gl_ref[at] = split(g)

    out_ref[...] = (x * math.sqrt(rows)).astype(bf16)


def vmem(count):
    return [pl.BlockSpec(memory_space=pltpu.VMEM)] * count


PARAMS = pltpu.CompilerParams(vmem_limit_bytes=40 * 1024 * 1024)


def after(value, *earlier):
    return lax.optimization_barrier((value, *earlier))[0]


def on_device(grad_parts, momentum):
    dp = lax.axis_index("dp")
    tensor = lax.axis_index("tensor")
    y, z = dp >> 2, dp & 3
    x, core = tensor >> 2, tensor & 1
    _, experts, rows, cols = grad_parts.shape
    half = rows // 2
    parts = grad_parts[0].reshape(NY, NZ, rows, cols)

    bottom, top = slice(half, rows), slice(0, half)

    def pick(k, piece):
        found = []
        for zk, span in piece:
            start = ((y + k) & 3, (z + zk) & 3, span.start, 0)
            found.append(lax.dynamic_slice(parts, start, (1, 1, span.stop - span.start, cols))[0, 0])
        return found[0] if len(found) == 1 else jnp.concatenate(found, axis=0)

    def total(piece, received):
        value = pick(0, piece).astype(f32)
        for other in received:
            value = value + other.astype(f32)
        return value

    whole = slice(0, rows)
    stages = [((2, whole),), ((1, bottom), (3, top)), ((1, top), (3, bottom)), ((0, whole),)]
    got = []
    received = ()
    for n, piece in enumerate(stages):
        pieces = [pick(k, piece) for k in (1, 3, 2)]
        outgoing = ()
        if n > 0:
            value = total(stages[n - 1], received)
            if n == 3:
                value = value + jnp.concatenate(got[0], axis=0)
            outgoing = (value[:half], value[half:])
        pieces, outgoing, got, received = lax.optimization_barrier((pieces, outgoing, got, received))
        received = [to_y(value, k) for value, k in zip(pieces, (1, 3, 2))]
        if n > 0:
            got = [*got, [to_z(outgoing[0], 1), to_z(outgoing[1], 3)]]
    own = total(stages[3], received)
    got_bottom, got_top = [got[1][0], got[2][1]], [got[2][0], got[1][1]]
    from_below = jnp.concatenate([got_top[0], got_bottom[0]], axis=0)
    from_above = jnp.concatenate([got_top[1], got_bottom[1]], axis=0)

    blended, new_momentum, gram = pl.pallas_call(
        gram_kernel,
        out_shape=(
            jax.ShapeDtypeStruct((rows, cols), f32),
            jax.ShapeDtypeStruct((rows, cols), bf16),
            jax.ShapeDtypeStruct((len(PAIRS), BLK, BLK), f32),
        ),
        in_specs=vmem(4),
        out_specs=tuple(vmem(3)),
        compiler_params=PARAMS,
    )(own, from_below, from_above, momentum[0])

    halves = gram.reshape(2, 3 * BLK, BLK)
    kept = lax.dynamic_index_in_dim(halves, core, 0, keepdims=False)
    kept = kept + lax.ppermute(lax.dynamic_index_in_dim(halves, 1 - core, 0, keepdims=False), "tensor", CORE_PERM)
    quarters = kept.reshape(NX, 3 * BLK // NX, BLK)

    def quarter(k):
        return lax.dynamic_index_in_dim(quarters, (x + k) & 3, 0, keepdims=False)

    received = [to_x(quarter(k), k) for k in (2, 1, 3)]
    piece = quarter(0) + received[0] + (received[1] + received[2])
    piece = piece + lax.ppermute(piece, "tensor", ZLO_PERM)
    gathered = jnp.zeros_like(quarters)
    gathered = lax.dynamic_update_index_in_dim(gathered, piece, x, 0)
    for k in (2, 1, 3):
        gathered = lax.dynamic_update_index_in_dim(gathered, to_x(piece, k), (x - k) & 3, 0)
    mine = gathered.reshape(3, BLK, BLK)
    other = lax.ppermute(mine, "tensor", CORE_PERM)

    size = 3 * BLK
    update = pl.pallas_call(
        lambda *refs: chain_kernel(rows * 16, *refs),
        out_shape=jax.ShapeDtypeStruct((rows, cols), bf16),
        in_specs=[pl.BlockSpec(memory_space=pltpu.SMEM)] + vmem(3),
        out_specs=vmem(1)[0],
        scratch_shapes=[pltpu.VMEM((size, size), f32)] + [pltpu.VMEM((size, size), bf16)] * 6,
        compiler_params=PARAMS,
    )(core.reshape(1).astype(jnp.int32), mine, other, blended)

    out = jnp.zeros((NY, NZ, rows, cols), bf16)

    def put(out, value, ky, kz, row):
        return lax.dynamic_update_slice(out, value[None, None], ((y + ky) & 3, (z + kz) & 3, row, 0))

    z_below, z_above = to_z(update, 1), to_z(update, 3)
    below, above = to_y(update, 1), to_y(update, 3)
    far_top, far_bottom = to_y(below[:half], 1), to_y(above[half:], 3)
    sides = jnp.concatenate([z_below, z_above], axis=0)
    z_far_top, z_far_bottom = to_z(z_below[:half], 1), to_z(z_above[half:], 3)
    sides_below, sides_above = to_y(sides, 1), to_y(sides, 3)
    z_far = jnp.concatenate([z_far_top, z_far_bottom], axis=0)
    z_far_below, z_far_above = to_y(z_far, 1), to_y(z_far, 3)
    sides_top = to_y(jnp.concatenate([sides_below[:half], sides_below[rows:rows + half]], axis=0), 1)
    sides_bottom = to_y(jnp.concatenate([sides_above[half:rows], sides_above[rows + half:]], axis=0), 3)
    z_far_far_top, z_far_far_bottom = to_y(z_far_below[:half], 1), to_y(z_far_above[half:], 3)

    out = put(out, update, 0, 0, 0)
    out = put(out, below, -1, 0, 0)
    out = put(out, above, 1, 0, 0)
    out = put(out, far_top, 2, 0, 0)
    out = put(out, far_bottom, 2, 0, half)
    for n, kz in enumerate((-1, 1)):
        at = slice(n * rows, (n + 1) * rows)
        out = put(out, sides[at], 0, kz, 0)
        out = put(out, sides_below[at], -1, kz, 0)
        out = put(out, sides_above[at], 1, kz, 0)
    out = put(out, z_far, 0, 2, 0)
    out = put(out, z_far_below, -1, 2, 0)
    out = put(out, z_far_above, 1, 2, 0)
    for n, kz in enumerate((-1, 1)):
        at = slice(n * half, (n + 1) * half)
        out = put(out, sides_top[at], 2, kz, 0)
        out = put(out, sides_bottom[at], 2, kz, half)
    out = put(out, z_far_far_top, 2, 2, 0)
    out = put(out, z_far_far_bottom, 2, 2, half)
    return (out.reshape(experts, rows, cols), new_momentum[None])


def solution(mesh):
    return jax.shard_map(
        on_device,
        mesh=mesh,
        in_specs=(P("dp", None, "tensor", None), P("dp", "tensor", None)),
        out_specs=(P(None, "tensor", None), P("dp", "tensor", None)),
        check_vma=False,
    )
```

```python
import math

import jax
import jax.numpy as jnp
from jax import lax
from jax.experimental import pallas as pl
from jax.experimental.pallas import tpu as pltpu
from jax.sharding import PartitionSpec as P

ITERS = 3
NY, NZ = 4, 4
NX = 4

momentum_decay = 0.95
epsilon = 1e-07
first_coef = 3.4445
third_coef = -4.775
fifth_coef = 2.0315
f32 = jnp.float32
bf16 = jnp.bfloat16
BLK = 256
PAIRS = ((0, 0), (0, 1), (1, 1), (0, 2), (1, 2), (2, 2))

Y_PERM = {k: [(y * NZ + z, (y + k) % NY * NZ + z) for y in range(NY) for z in range(NZ)] for k in (1, 2, 3)}
X_PERM = {k: [(t, (t + 4 * k) % 16) for t in range(16)] for k in (1, 2, 3)}
CORE_PAIRS = [(t, t ^ 1) for t in range(16)]
ZLO_PAIRS = [(t, t ^ 2) for t in range(16)]


def z_pairs(first):
    pairs = []
    for dp in range(NY * NZ):
        for t in range(16):
            other = dp ^ (1 if (t % 2 == 0) == first else 3)
            pairs.append((dp * 16 + t, other * 16 + t))
    return pairs


Z_PAIRS = {first: z_pairs(first) for first in (True, False)}


def to_y(value, k):
    return lax.ppermute(value, "dp", Y_PERM[k])


def to_x(value, k):
    return lax.ppermute(value, "tensor", X_PERM[k])


def swap_z(value, first):
    return lax.ppermute(value, ("dp", "tensor"), Z_PAIRS[first])


def split(value):
    hi = value.astype(bf16)
    lo = (value - hi.astype(f32)).astype(bf16)
    return hi, lo


def product(a, b, axis=1):
    left = jnp.concatenate([a[0], a[0], a[1]], axis=axis)
    right = jnp.concatenate([b[0], b[1], b[0]], axis=0)
    return lax.dot_general(left, right, (((axis,), (0,)), ((), ())), preferred_element_type=f32)


def block(n):
    return slice(n * BLK, (n + 1) * BLK)


def gram_kernel(s_ref, m_ref, b_ref, nm_ref, g_ref):
    summed = s_ref[...]
    velocity = momentum_decay * m_ref[...].astype(f32) + summed
    nm_ref[...] = velocity.astype(bf16)
    blended = summed + momentum_decay * velocity
    b_ref[...] = blended
    hi, lo = split(blended)
    for n, (i, j) in enumerate(PAIRS):
        at, to = block(i), block(j)
        g_ref[n] = product((hi[:, at], lo[:, at]), (hi[:, to], lo[:, to]), 0)


def chain_kernel(rows, c_ref, mine_ref, other_ref, b_ref, out_ref, g_ref, gh_ref, gl_ref, qh_ref, ql_ref, sh_ref, sl_ref):
    g, q, s = (gh_ref, gl_ref), (qh_ref, ql_ref), (sh_ref, sl_ref)
    diagonal = lax.broadcasted_iota(jnp.int32, (BLK, BLK), 0) == lax.broadcasted_iota(jnp.int32, (BLK, BLK), 1)

    def store(refs, i, j, value):
        for ref, part in zip(refs, split(value)):
            ref[block(i), block(j)] = part
            if i != j:
                ref[block(j), block(i)] = part.T

    def upper(a, b, use):
        for i in range(3):
            strip = product([ref[block(i)] for ref in a], [ref[:, i * BLK:] for ref in b])
            for j in range(i, 3):
                use(i, j, strip[:, block(j - i)])

    def store_q(i, j, squared):
        value = third_coef * g_ref[block(i), block(j)] + fifth_coef * squared
        store(q, i, j, value + jnp.where(diagonal, first_coef, 0.0) if i == j else value)

    def store_s(i, j, value):
        store(s, i, j, value)

    def store_g(i, j, value):
        g_ref[block(i), block(j)] = value
        store(g, i, j, value)

    first = c_ref[0] == 0
    blocks = []
    trace = jnp.zeros((1, 1), f32)
    for n, (i, j) in enumerate(PAIRS):
        mine, other = mine_ref[n % 3], other_ref[n % 3]
        blocks.append(jnp.where(first, mine, other) if n < 3 else jnp.where(first, other, mine))
        if i == j:
            trace += jnp.sum(jnp.where(diagonal, blocks[n], 0.0), keepdims=True)
    inverse = 1.0 / (jnp.sqrt(trace) + epsilon)
    squared_inverse = inverse * inverse
    for n, (i, j) in enumerate(PAIRS):
        store_g(i, j, blocks[n] * squared_inverse)
    x = b_ref[...] * inverse
    for iteration in range(ITERS):
        upper(g, g, store_q)
        x = product(split(x), [ref[...] for ref in q])
        if iteration < ITERS - 1:
            upper(g, q, store_s)
            upper(s, q, store_g)
    out_ref[...] = (x * math.sqrt(rows)).astype(bf16)


def vmem(count):
    return [pl.BlockSpec(memory_space=pltpu.VMEM)] * count


PARAMS = pltpu.CompilerParams(vmem_limit_bytes=40 * 1024 * 1024)


def after(value, *earlier):
    return lax.optimization_barrier((value, *earlier))[0]


def on_device(grad_parts, momentum):
    dp = lax.axis_index("dp")
    tensor = lax.axis_index("tensor")
    y, z = dp >> 2, dp & 3
    x, core = tensor >> 2, tensor & 1
    _, experts, rows, cols = grad_parts.shape
    parts = grad_parts[0].reshape(NY, NZ, rows, cols)
    a, b = 1 + 2 * core, 3 - 2 * core

    def partial(source, ky, kz):
        return lax.dynamic_slice(source, ((y + ky) & 3, z ^ kz, 0, 0), (1, 1, rows, cols))[0, 0]

    columns = (2, a, b, 0)
    outgoing = [partial(parts, ky, columns[0]) for ky in (2, 1, 3)]
    parts = after(parts, outgoing)
    moved, arrived = [], []
    for n, kz in enumerate(columns):
        if n > 0:
            outgoing = after([partial(parts, ky, kz) for ky in (2, 1, 3)], *arrived)
        arrived = [to_y(piece, ky) for piece, ky in zip(outgoing, (2, 1, 3))]
        value = partial(after(parts, *arrived), 0, kz).astype(f32)
        for other in after(arrived, *moved) + [[], [], moved[:1], moved[1:]][n]:
            value = value + other.astype(f32)
        if n < 3:
            moved.append(swap_z(value, n < 2))

    blended, new_momentum, gram = pl.pallas_call(
        gram_kernel,
        out_shape=(
            jax.ShapeDtypeStruct((rows, cols), f32),
            jax.ShapeDtypeStruct((rows, cols), bf16),
            jax.ShapeDtypeStruct((len(PAIRS), BLK, BLK), f32),
        ),
        in_specs=vmem(2),
        out_specs=tuple(vmem(3)),
        compiler_params=PARAMS,
    )(value, momentum[0])

    halves = gram.reshape(2, 3 * BLK, BLK)
    kept = lax.dynamic_index_in_dim(halves, core, 0, keepdims=False)
    kept = kept + lax.ppermute(lax.dynamic_index_in_dim(halves, 1 - core, 0, keepdims=False), "tensor", CORE_PAIRS)
    quarters = kept.reshape(NX, 3 * BLK // NX, BLK)

    def quarter(k):
        return lax.dynamic_index_in_dim(quarters, (x + k) & 3, 0, keepdims=False)

    received = [to_x(quarter(k), k) for k in (2, 1, 3)]
    piece = quarter(0) + received[0] + (received[1] + received[2])
    piece = piece + lax.ppermute(piece, "tensor", ZLO_PAIRS)
    gathered = jnp.zeros_like(quarters)
    gathered = lax.dynamic_update_index_in_dim(gathered, piece, x, 0)
    for k in (2, 1, 3):
        gathered = lax.dynamic_update_index_in_dim(gathered, to_x(piece, k), (x - k) & 3, 0)
    mine = gathered.reshape(3, BLK, BLK)
    other = lax.ppermute(mine, "tensor", CORE_PAIRS)

    size = 3 * BLK
    update = pl.pallas_call(
        lambda *refs: chain_kernel(rows * 16, *refs),
        out_shape=jax.ShapeDtypeStruct((rows, cols), bf16),
        in_specs=[pl.BlockSpec(memory_space=pltpu.SMEM)] + vmem(3),
        out_specs=vmem(1)[0],
        scratch_shapes=[pltpu.VMEM((size, size), f32)] + [pltpu.VMEM((size, size), bf16)] * 6,
        compiler_params=PARAMS,
    )(core.reshape(1).astype(jnp.int32), mine, other, blended)

    out = jnp.zeros((NY, NZ, rows, cols), bf16)
    half = rows // 2

    def put(out, value, ky, kz, row):
        return lax.dynamic_update_slice(out, value[None, None], ((y + ky) & 3, z ^ kz, row, 0))

    def sides(value):
        return to_y(value, 1), to_y(value, 3)

    def relays(value_sides):
        (below, above), count = value_sides, value_sides[0].shape[0] // rows
        top = jnp.concatenate([below[n * rows:n * rows + half] for n in range(count)], axis=0)
        bottom = jnp.concatenate([above[n * rows + half:(n + 1) * rows] for n in range(count)], axis=0)
        return to_y(top, 1), to_y(bottom, 3)

    z_a = swap_z(update, True)
    own_sides = sides(update)
    z_rest = swap_z(jnp.concatenate([update, z_a], axis=0), False)
    a_sides = sides(z_a)
    near_sides = [jnp.concatenate(pair, axis=0) for pair in zip(own_sides, a_sides)]
    near_relays = relays(near_sides)
    rest_sides = sides(z_rest)
    far_relays = relays(rest_sides)
    for found, found_sides, relayed, columns in (
        ([update, z_a], near_sides, near_relays, (0, a)),
        ([z_rest[:rows], z_rest[rows:]], rest_sides, far_relays, (b, 2)),
    ):
        for n, kz in enumerate(columns):
            at, part = slice(n * rows, (n + 1) * rows), slice(n * half, (n + 1) * half)
            out = put(out, found[n], 0, kz, 0)
            out = put(out, found_sides[0][at], -1, kz, 0)
            out = put(out, found_sides[1][at], 1, kz, 0)
            out = put(out, relayed[0][part], 2, kz, 0)
            out = put(out, relayed[1][part], 2, kz, half)
    return (out.reshape(experts, rows, cols), new_momentum[None])


def solution(mesh):
    return jax.shard_map(
        on_device,
        mesh=mesh,
        in_specs=(P("dp", None, "tensor", None), P("dp", "tensor", None)),
        out_specs=(P(None, "tensor", None), P("dp", "tensor", None)),
        check_vma=False,
    )
```

```python
import math

import jax
import jax.numpy as jnp
from jax import lax
from jax.experimental import pallas as pl
from jax.experimental.pallas import tpu as pltpu
from jax.sharding import PartitionSpec as P

ITERS = 3
NY, NZ = 4, 4
NX = 4

momentum_decay = 0.95
epsilon = 1e-07
first_coef = 3.4445
third_coef = -4.775
fifth_coef = 2.0315
f32 = jnp.float32
bf16 = jnp.bfloat16
BLK = 256
PAIRS = ((0, 0), (0, 1), (1, 1), (0, 2), (1, 2), (2, 2))

Y_PERM = {k: [(y * NZ + z, (y + k) % NY * NZ + z) for y in range(NY) for z in range(NZ)] for k in (1, 2, 3)}
X_PERM = {k: [(t, (t + 4 * k) % 16) for t in range(16)] for k in (1, 2, 3)}
CORE_PAIRS = [(t, t ^ 1) for t in range(16)]
ZLO_PAIRS = [(t, t ^ 2) for t in range(16)]


def z_pairs(first):
    pairs = []
    for dp in range(NY * NZ):
        for t in range(16):
            other = dp ^ (1 if (t % 2 == 0) == first else 3)
            pairs.append((dp * 16 + t, other * 16 + t))
    return pairs


Z_PAIRS = {first: z_pairs(first) for first in (True, False)}


def to_y(value, k):
    return lax.ppermute(value, "dp", Y_PERM[k])


def to_x(value, k):
    return lax.ppermute(value, "tensor", X_PERM[k])


def swap_z(value, first):
    return lax.ppermute(value, ("dp", "tensor"), Z_PAIRS[first])


def split(value):
    hi = value.astype(bf16)
    lo = (value - hi.astype(f32)).astype(bf16)
    return hi, lo


def product(a, b, axis=1):
    left = jnp.concatenate([a[0], a[0], a[1]], axis=axis)
    right = jnp.concatenate([b[0], b[1], b[0]], axis=0)
    return lax.dot_general(left, right, (((axis,), (0,)), ((), ())), preferred_element_type=f32)


def block(n):
    return slice(n * BLK, (n + 1) * BLK)


def gram_kernel(s_ref, m_ref, b_ref, nm_ref, g_ref):
    summed = s_ref[...]
    velocity = momentum_decay * m_ref[...].astype(f32) + summed
    nm_ref[...] = velocity.astype(bf16)
    blended = summed + momentum_decay * velocity
    b_ref[...] = blended
    hi, lo = split(blended)
    for n, (i, j) in enumerate(PAIRS):
        at, to = block(i), block(j)
        g_ref[n] = product((hi[:, at], lo[:, at]), (hi[:, to], lo[:, to]), 0)


def chain_kernel(rows, c_ref, mine_ref, other_ref, b_ref, out_ref, g_ref, gh_ref, gl_ref, qh_ref, ql_ref, sh_ref, sl_ref):
    g, q, s = (gh_ref, gl_ref), (qh_ref, ql_ref), (sh_ref, sl_ref)
    diagonal = lax.broadcasted_iota(jnp.int32, (BLK, BLK), 0) == lax.broadcasted_iota(jnp.int32, (BLK, BLK), 1)

    def store(refs, i, j, value):
        for ref, part in zip(refs, split(value)):
            ref[block(i), block(j)] = part
            if i != j:
                ref[block(j), block(i)] = part.T

    def upper(a, b, use):
        for i in range(3):
            strip = product([ref[block(i)] for ref in a], [ref[:, i * BLK:] for ref in b])
            for j in range(i, 3):
                use(i, j, strip[:, block(j - i)])

    def store_q(i, j, squared):
        value = third_coef * g_ref[block(i), block(j)] + fifth_coef * squared
        store(q, i, j, value + jnp.where(diagonal, first_coef, 0.0) if i == j else value)

    def store_s(i, j, value):
        store(s, i, j, value)

    def store_g(i, j, value):
        g_ref[block(i), block(j)] = value
        store(g, i, j, value)

    first = c_ref[0] == 0
    blocks = []
    trace = jnp.zeros((1, 1), f32)
    for n, (i, j) in enumerate(PAIRS):
        mine, other = mine_ref[n % 3], other_ref[n % 3]
        blocks.append(jnp.where(first, mine, other) if n < 3 else jnp.where(first, other, mine))
        if i == j:
            trace += jnp.sum(jnp.where(diagonal, blocks[n], 0.0), keepdims=True)
    inverse = 1.0 / (jnp.sqrt(trace) + epsilon)
    squared_inverse = inverse * inverse
    for n, (i, j) in enumerate(PAIRS):
        store_g(i, j, blocks[n] * squared_inverse)
    x = b_ref[...] * inverse
    for iteration in range(ITERS - 1):
        upper(g, g, store_q)
        x = product(split(x), [ref[...] for ref in q])
        upper(g, q, store_s)
        upper(s, q, store_g)
    last = [ref[...] for ref in g]
    once = product(split(x), last)
    x = first_coef * x + (third_coef * once + fifth_coef * product(split(once), last))
    out_ref[...] = (x * math.sqrt(rows)).astype(bf16)


def vmem(count):
    return [pl.BlockSpec(memory_space=pltpu.VMEM)] * count


PARAMS = pltpu.CompilerParams(vmem_limit_bytes=40 * 1024 * 1024)


def after(value, *earlier):
    return lax.optimization_barrier((value, *earlier))[0]


def on_device(grad_parts, momentum):
    dp = lax.axis_index("dp")
    tensor = lax.axis_index("tensor")
    y, z = dp >> 2, dp & 3
    x, core = tensor >> 2, tensor & 1
    _, experts, rows, cols = grad_parts.shape
    parts = grad_parts[0].reshape(NY, NZ, rows, cols)
    a, b = 1 + 2 * core, 3 - 2 * core

    def partial(source, ky, kz):
        return lax.dynamic_slice(source, ((y + ky) & 3, z ^ kz, 0, 0), (1, 1, rows, cols))[0, 0]

    columns = (2, a, b, 0)
    outgoing = [[partial(parts, ky, columns[0]) for ky in (2, 1, 3)]]
    parts = after(parts, outgoing)
    outgoing += [[partial(parts, ky, kz) for ky in (2, 1, 3)] for kz in columns[1:]]
    moved, arrived = [], []
    for n, kz in enumerate(columns):
        pieces = after(outgoing[n], *arrived) if n > 0 else outgoing[n]
        arrived = [to_y(piece, ky) for piece, ky in zip(pieces, (2, 1, 3))]
        value = partial(after(parts, *arrived), 0, kz).astype(f32)
        for other in after(arrived, *moved, *outgoing) + [[], [], moved[:1], moved[1:]][n]:
            value = value + other.astype(f32)
        if n < 3:
            moved.append(swap_z(value, n < 2))

    blended, new_momentum, gram = pl.pallas_call(
        gram_kernel,
        out_shape=(
            jax.ShapeDtypeStruct((rows, cols), f32),
            jax.ShapeDtypeStruct((rows, cols), bf16),
            jax.ShapeDtypeStruct((len(PAIRS), BLK, BLK), f32),
        ),
        in_specs=vmem(2),
        out_specs=tuple(vmem(3)),
        compiler_params=PARAMS,
    )(value, momentum[0])

    halves = gram.reshape(2, 3 * BLK, BLK)
    kept = lax.dynamic_index_in_dim(halves, core, 0, keepdims=False)
    kept = kept + lax.ppermute(lax.dynamic_index_in_dim(halves, 1 - core, 0, keepdims=False), "tensor", CORE_PAIRS)
    quarters = kept.reshape(NX, 3 * BLK // NX, BLK)

    def quarter(k):
        return lax.dynamic_index_in_dim(quarters, (x + k) & 3, 0, keepdims=False)

    received = [to_x(quarter(k), k) for k in (2, 1, 3)]
    piece = quarter(0) + received[0] + (received[1] + received[2])
    piece = piece + lax.ppermute(piece, "tensor", ZLO_PAIRS)
    gathered = jnp.zeros_like(quarters)
    gathered = lax.dynamic_update_index_in_dim(gathered, piece, x, 0)
    for k in (2, 1, 3):
        gathered = lax.dynamic_update_index_in_dim(gathered, to_x(piece, k), (x - k) & 3, 0)
    mine = gathered.reshape(3, BLK, BLK)
    other = lax.ppermute(mine, "tensor", CORE_PAIRS)

    size = 3 * BLK
    update = pl.pallas_call(
        lambda *refs: chain_kernel(rows * 16, *refs),
        out_shape=jax.ShapeDtypeStruct((rows, cols), bf16),
        in_specs=[pl.BlockSpec(memory_space=pltpu.SMEM)] + vmem(3),
        out_specs=vmem(1)[0],
        scratch_shapes=[pltpu.VMEM((size, size), f32)] + [pltpu.VMEM((size, size), bf16)] * 6,
        compiler_params=PARAMS,
    )(core.reshape(1).astype(jnp.int32), mine, other, blended)

    out = jnp.zeros((NY, NZ, rows, cols), bf16)
    half = rows // 2

    def put(out, value, ky, kz, row):
        return lax.dynamic_update_slice(out, value[None, None], ((y + ky) & 3, z ^ kz, row, 0))

    def sides(value):
        return to_y(value, 1), to_y(value, 3)

    def relays(value_sides):
        (below, above), count = value_sides, value_sides[0].shape[0] // rows
        top = jnp.concatenate([below[n * rows:n * rows + half] for n in range(count)], axis=0)
        bottom = jnp.concatenate([above[n * rows + half:(n + 1) * rows] for n in range(count)], axis=0)
        return to_y(top, 1), to_y(bottom, 3)

    z_a, z_b = swap_z(update, True), swap_z(update, False)
    own_sides = sides(update)
    own_relays = relays(own_sides)
    own_relays, z_a, z_b = lax.optimization_barrier((own_relays, z_a, z_b))
    z_2 = swap_z(z_a, False)
    z_near = jnp.concatenate([z_a, z_b], axis=0)
    near_sides = sides(z_near)
    far_sides = sides(z_2)
    near_relays = relays(near_sides)
    far_relays = relays(far_sides)
    for found, found_sides, relayed, columns in (
        (update, own_sides, own_relays, (0,)),
        (z_near, near_sides, near_relays, (a, b)),
        (z_2, far_sides, far_relays, (2,)),
    ):
        for n, kz in enumerate(columns):
            at, part = slice(n * rows, (n + 1) * rows), slice(n * half, (n + 1) * half)
            out = put(out, found[at], 0, kz, 0)
            out = put(out, found_sides[0][at], -1, kz, 0)
            out = put(out, found_sides[1][at], 1, kz, 0)
            out = put(out, relayed[0][part], 2, kz, 0)
            out = put(out, relayed[1][part], 2, kz, half)
    return (out.reshape(experts, rows, cols), new_momentum[None])


def solution(mesh):
    return jax.shard_map(
        on_device,
        mesh=mesh,
        in_specs=(P("dp", None, "tensor", None), P("dp", "tensor", None)),
        out_specs=(P(None, "tensor", None), P("dp", "tensor", None)),
        check_vma=False,
    )
```

```python
import math

import jax
import jax.numpy as jnp
from jax import lax
from jax.experimental import pallas as pl
from jax.experimental.pallas import tpu as pltpu
from jax.sharding import PartitionSpec as P

ITERS = 3
NY, NZ = 4, 4
NX = 4

momentum_decay = 0.95
epsilon = 1e-07
first_coef = 3.4445
third_coef = -4.775
fifth_coef = 2.0315
f32 = jnp.float32
bf16 = jnp.bfloat16
BLK = 256
PAIRS = ((0, 0), (0, 1), (1, 1), (0, 2), (1, 2), (2, 2))

Y_PERM = {k: [(y * NZ + z, (y + k) % NY * NZ + z) for y in range(NY) for z in range(NZ)] for k in (1, 2, 3)}
X_PERM = {k: [(t, (t + 4 * k) % 16) for t in range(16)] for k in (1, 2, 3)}
CORE_PAIRS = [(t, t ^ 1) for t in range(16)]
ZLO_PAIRS = [(t, t ^ 2) for t in range(16)]


def z_pairs(first):
    pairs = []
    for dp in range(NY * NZ):
        for t in range(16):
            other = dp ^ (1 if (t % 2 == 0) == first else 3)
            pairs.append((dp * 16 + t, other * 16 + t))
    return pairs


Z_PAIRS = {first: z_pairs(first) for first in (True, False)}


def to_y(value, k):
    return lax.ppermute(value, "dp", Y_PERM[k])


def to_x(value, k):
    return lax.ppermute(value, "tensor", X_PERM[k])


def swap_z(value, first):
    return lax.ppermute(value, ("dp", "tensor"), Z_PAIRS[first])


def split(value):
    hi = value.astype(bf16)
    lo = (value - hi.astype(f32)).astype(bf16)
    return hi, lo


def product(a, b, axis=1):
    left = jnp.concatenate([a[0], a[0], a[1]], axis=axis)
    right = jnp.concatenate([b[0], b[1], b[0]], axis=0)
    return lax.dot_general(left, right, (((axis,), (0,)), ((), ())), preferred_element_type=f32)


def block(n):
    return slice(n * BLK, (n + 1) * BLK)


def gram_kernel(s_ref, m_ref, b_ref, nm_ref, g_ref):
    summed = s_ref[...]
    velocity = momentum_decay * m_ref[...].astype(f32) + summed
    nm_ref[...] = velocity.astype(bf16)
    blended = summed + momentum_decay * velocity
    b_ref[...] = blended
    hi, lo = split(blended)
    for n, (i, j) in enumerate(PAIRS):
        at, to = block(i), block(j)
        g_ref[n] = product((hi[:, at], lo[:, at]), (hi[:, to], lo[:, to]), 0)


def chain_kernel(rows, c_ref, mine_ref, other_ref, b_ref, out_ref, g_ref, gh_ref, gl_ref, qh_ref, ql_ref, sh_ref, sl_ref):
    g, q, s = (gh_ref, gl_ref), (qh_ref, ql_ref), (sh_ref, sl_ref)
    diagonal = lax.broadcasted_iota(jnp.int32, (BLK, BLK), 0) == lax.broadcasted_iota(jnp.int32, (BLK, BLK), 1)

    def store(refs, i, j, value):
        for ref, part in zip(refs, split(value)):
            ref[block(i), block(j)] = part
            if i != j:
                ref[block(j), block(i)] = part.T

    def upper(a, b, use):
        for i in range(3):
            strip = product([ref[block(i)] for ref in a], [ref[:, i * BLK:] for ref in b])
            for j in range(i, 3):
                use(i, j, strip[:, block(j - i)])

    def store_q(i, j, squared):
        value = third_coef * g_ref[block(i), block(j)] + fifth_coef * squared
        store(q, i, j, value + jnp.where(diagonal, first_coef, 0.0) if i == j else value)

    def store_s(i, j, value):
        store(s, i, j, value)

    def store_g(i, j, value):
        g_ref[block(i), block(j)] = value
        store(g, i, j, value)

    first = c_ref[0] == 0
    blocks = []
    trace = jnp.zeros((1, 1), f32)
    for n, (i, j) in enumerate(PAIRS):
        mine, other = mine_ref[n % 3], other_ref[n % 3]
        blocks.append(jnp.where(first, mine, other) if n < 3 else jnp.where(first, other, mine))
        if i == j:
            trace += jnp.sum(jnp.where(diagonal, blocks[n], 0.0), keepdims=True)
    inverse = 1.0 / (jnp.sqrt(trace) + epsilon)
    squared_inverse = inverse * inverse
    for n, (i, j) in enumerate(PAIRS):
        store_g(i, j, blocks[n] * squared_inverse)
    x = b_ref[...] * inverse
    for iteration in range(ITERS - 1):
        upper(g, g, store_q)
        x = product(split(x), [ref[...] for ref in q])
        upper(g, q, store_s)
        upper(s, q, store_g)
    last = [ref[...] for ref in g]
    once = product(split(x), last)
    x = first_coef * x + (third_coef * once + fifth_coef * product(split(once), last))
    out_ref[...] = (x * math.sqrt(rows)).astype(bf16)


def vmem(count):
    return [pl.BlockSpec(memory_space=pltpu.VMEM)] * count


PARAMS = pltpu.CompilerParams(vmem_limit_bytes=40 * 1024 * 1024)


def after(value, *earlier):
    return lax.optimization_barrier((value, *earlier))[0]


def on_device(grad_parts, momentum):
    dp = lax.axis_index("dp")
    tensor = lax.axis_index("tensor")
    y, z = dp >> 2, dp & 3
    x, core = tensor >> 2, tensor & 1
    _, experts, rows, cols = grad_parts.shape
    parts = grad_parts[0].reshape(NY, NZ, rows, cols)
    a, b = 1 + 2 * core, 3 - 2 * core

    def partial(source, ky, kz):
        return lax.dynamic_slice(source, ((y + ky) & 3, z ^ kz, 0, 0), (1, 1, rows, cols))[0, 0]

    columns = (2, a, b, 0)
    outgoing = [[partial(parts, ky, columns[0]) for ky in (2, 1, 3)]]
    parts = after(parts, outgoing)
    outgoing += [[partial(parts, ky, kz) for ky in (2, 1, 3)] for kz in columns[1:]]
    middle = rows // 2
    tops, bottoms, arrived = [], [], []
    for n, kz in enumerate(columns):
        pieces = after(outgoing[n], *arrived, *bottoms[:max(n - 1, 0)]) if n > 0 else outgoing[n]
        arrived = [to_y(piece, ky) for piece, ky in zip(pieces, (2, 1, 3))]
        value = partial(after(parts, *arrived), 0, kz).astype(f32)
        moved = [jnp.concatenate(pair, axis=0) for pair in zip(tops, bottoms)]
        for other in after(arrived, *tops, *outgoing) + [[], [], moved[:1], moved[1:]][n]:
            value = value + other.astype(f32)
        if n < 3:
            tops.append(swap_z(value[:middle], n < 2))
            bottoms.append(swap_z(value[middle:], n < 2))

    blended, new_momentum, gram = pl.pallas_call(
        gram_kernel,
        out_shape=(
            jax.ShapeDtypeStruct((rows, cols), f32),
            jax.ShapeDtypeStruct((rows, cols), bf16),
            jax.ShapeDtypeStruct((len(PAIRS), BLK, BLK), f32),
        ),
        in_specs=vmem(2),
        out_specs=tuple(vmem(3)),
        compiler_params=PARAMS,
    )(value, momentum[0])

    halves = gram.reshape(2, NX, 3 * BLK // NX, BLK)
    other = lax.ppermute(lax.dynamic_index_in_dim(halves, 1 - core, 0, keepdims=False), "tensor", CORE_PAIRS)

    def quarter(k):
        at = (x + k) & 3
        mine = lax.dynamic_slice(halves, (core, at, 0, 0), (1, 1, *halves.shape[2:]))[0, 0]
        return mine + lax.dynamic_index_in_dim(other, at, 0, keepdims=False)

    received = [to_x(quarter(k), k) for k in (2, 1, 3)]
    piece = quarter(0) + received[0] + (received[1] + received[2])
    piece = piece + lax.ppermute(piece, "tensor", ZLO_PAIRS)
    gathered = jnp.zeros_like(other)
    gathered = lax.dynamic_update_index_in_dim(gathered, piece, x, 0)
    for k in (2, 1, 3):
        gathered = lax.dynamic_update_index_in_dim(gathered, to_x(piece, k), (x - k) & 3, 0)
    mine = gathered.reshape(3, BLK, BLK)
    other = lax.ppermute(mine, "tensor", CORE_PAIRS)

    size = 3 * BLK
    update = pl.pallas_call(
        lambda *refs: chain_kernel(rows * 16, *refs),
        out_shape=jax.ShapeDtypeStruct((rows, cols), bf16),
        in_specs=[pl.BlockSpec(memory_space=pltpu.SMEM)] + vmem(3),
        out_specs=vmem(1)[0],
        scratch_shapes=[pltpu.VMEM((size, size), f32)] + [pltpu.VMEM((size, size), bf16)] * 6,
        compiler_params=PARAMS,
    )(core.reshape(1).astype(jnp.int32), mine, other, blended)

    out = jnp.zeros((NY, NZ, rows, cols), bf16)
    half = rows // 2

    def put(out, value, ky, kz, row):
        return lax.dynamic_update_slice(out, value[None, None], ((y + ky) & 3, z ^ kz, row, 0))

    def sides(value):
        return to_y(value, 1), to_y(value, 3)

    def relays(value_sides):
        (below, above), count = value_sides, value_sides[0].shape[0] // rows
        top = jnp.concatenate([below[n * rows:n * rows + half] for n in range(count)], axis=0)
        bottom = jnp.concatenate([above[n * rows + half:(n + 1) * rows] for n in range(count)], axis=0)
        return to_y(top, 1), to_y(bottom, 3)

    z_a, z_b = swap_z(update, True), swap_z(update, False)
    own_sides = sides(update)
    own_relays = relays(own_sides)
    own_relays, z_a, z_b = lax.optimization_barrier((own_relays, z_a, z_b))
    z_2 = swap_z(z_a, False)
    z_near = jnp.concatenate([z_a, z_b], axis=0)
    near_sides = sides(z_near)
    far_sides = sides(z_2)
    near_relays = relays(near_sides)
    far_relays = relays(far_sides)
    for found, found_sides, relayed, columns in (
        (update, own_sides, own_relays, (0,)),
        (z_near, near_sides, near_relays, (a, b)),
        (z_2, far_sides, far_relays, (2,)),
    ):
        for n, kz in enumerate(columns):
            at, part = slice(n * rows, (n + 1) * rows), slice(n * half, (n + 1) * half)
            out = put(out, found[at], 0, kz, 0)
            out = put(out, found_sides[0][at], -1, kz, 0)
            out = put(out, found_sides[1][at], 1, kz, 0)
            out = put(out, relayed[0][part], 2, kz, 0)
            out = put(out, relayed[1][part], 2, kz, half)
    return (out.reshape(experts, rows, cols), new_momentum[None])


def solution(mesh):
    return jax.shard_map(
        on_device,
        mesh=mesh,
        in_specs=(P("dp", None, "tensor", None), P("dp", "tensor", None)),
        out_specs=(P(None, "tensor", None), P("dp", "tensor", None)),
        check_vma=False,
    )
```
